1024 devices in a mesh: row: 32 (over x, y, core), col: 32 (over z).
Axes of the slice: x: 4, y: 4, z: 32, core: 2. Of those that a mesh axis runs over, the one named last changes fastest.
Arguments:
- tokens: bfloat16 [512, 12288], P('row', 'col'), may hold values from -6 to 6
- w_in: bfloat16 [12288, 24576], P('col', 'row'), may hold values from -0.0546875 to 0.0546875
- w_out: bfloat16 [24576, 12288], P('row', 'col'), may hold values from -0.0390625 to 0.0390625
- cotangent: bfloat16 [512, 12288], P('row', 'col'), may hold values from -6 to 6
Outputs:
- output: bfloat16 [512, 12288], P('row', 'col')
- grad_tokens: bfloat16 [512, 12288], P('row', 'col')
- grad_in: float32 [12288, 24576], P('col', 'row')
- grad_out: float32 [24576, 12288], P('row', 'col')
The draws below stay inside these ranges and needn't reach their ends.
All inputs are finite; a program needn't handle non-finite values.
Results may differ from the reference program's by a relative error of at most 0.0033.
Values may be sent and summed in bfloat16 or wider, within the bound.
A program may use at most 32 MiB of HBM per device.

```python
import jax
import jax.numpy as jnp
from jax import lax

D = 12288
FF = 24576
TOKENS = 512


def block_levels(rng, shape, cuts, smallest, high):
    def one(dim, blocks):
        heights = jax.random.uniform(jax.random.fold_in(jax.random.fold_in(rng, 6), dim), (blocks,), jnp.float32, smallest / len(cuts), high / len(cuts))
        return jnp.repeat(jnp.exp(heights), shape[dim] // blocks).reshape((-1,) + (1,) * (len(shape) - dim - 1))

    level = one(*cuts[0])
    for cut in cuts[1:]:
        level = level * one(*cut)
    return level


def normal_values(stream_key, shape, width, reach, cuts=(), held_as=jnp.bfloat16):
    entries = jax.random.normal(stream_key, shape, jnp.float32) * width
    if len(cuts) > 0:
        entries = block_levels(stream_key, shape, cuts, -0.22, 0.18) * entries
    return jnp.clip(entries, min=-reach, max=reach).astype(held_as)


def setup_inputs(seed: int = 0) -> dict:
    streams_of = jax.random.split(jax.random.key(seed), 5)
    return {
        "tokens": normal_values(streams_of[0], (TOKENS, D), 1.0, 6.0, ((0, 32), (1, 32))),
        "w_in": normal_values(streams_of[1], (D, FF), D ** -0.5, 0.0546875, ((0, 32), (1, 32))),
        "w_out": normal_values(streams_of[2], (FF, D), FF ** -0.5, 0.0390625, ((0, 32), (1, 32))),
        "cotangent": normal_values(streams_of[3], (TOKENS, D), 1.0, 6.0, ((0, 32), (1, 32))),
    }


slope_c = 0.7978845608028654
cubic_k = 0.044715


def gelu_value(h):
    inner = slope_c * (h + cubic_k * h * h * h)
    return 0.5 * h * (1.0 + jnp.tanh(inner))


def gelu_slope(h):
    inner = slope_c * (h + cubic_k * h * h * h)
    tval = jnp.tanh(inner)
    return 0.5 * (1.0 + tval) + 0.5 * h * (1.0 - tval * tval) * slope_c * (1.0 + 3.0 * cubic_k * h * h)


def contract_first(left, right):
    return lax.dot_general(left, right, (((0,), (0,)), ((), ())), preferred_element_type=jnp.float32)


def contract_last(left, right):
    return lax.dot_general(left, right, (((1,), (1,)), ((), ())), preferred_element_type=jnp.float32)


def reference(tokens, w_in, w_out, cotangent):
    pre = jnp.dot(tokens, w_in, preferred_element_type=jnp.float32)
    act = gelu_value(pre).astype(jnp.bfloat16)
    output = (tokens.astype(jnp.float32) + jnp.dot(act, w_out, preferred_element_type=jnp.float32)).astype(jnp.bfloat16)
    dact = contract_last(cotangent, w_out)
    dpre = (dact * gelu_slope(pre)).astype(jnp.bfloat16)
    grad_out = contract_first(act, cotangent)
    grad_in = contract_first(tokens, dpre)
    grad_tokens = (cotangent.astype(jnp.float32) + contract_last(dpre, w_in)).astype(jnp.bfloat16)
    return output, grad_tokens, grad_in, grad_out
```

```python
import functools

import jax
import jax.numpy as jnp
from jax import lax
from jax.experimental import pallas as pl
from jax.experimental.pallas import tpu as pltpu
from jax.sharding import PartitionSpec as P

slope_c = 0.7978845608028654
cubic_k = 0.044715
MESH = pl.DeviceIdType.MESH
SCALE = 2.0**20
BF = jnp.bfloat16
F32 = jnp.float32


def gelu_both(h):
    tval = jnp.tanh(slope_c * (h + cubic_k * h * h * h))
    value = 0.5 * h * (1.0 + tval)
    slope = 0.5 * (1.0 + tval) + 0.5 * h * (1.0 - tval * tval) * slope_c * (
        1.0 + 3.0 * cubic_k * h * h
    )
    return value, slope


def encode(x):
    a = x * SCALE
    a = a * a
    a = a * a
    return jnp.where(x < 0.0, -a, a).astype(BF)


def decode(y):
    y = y.astype(F32)
    a = jnp.sqrt(jnp.sqrt(jnp.abs(y))) * (1.0 / SCALE)
    return jnp.where(y < 0.0, -a, a)


def mm(left, right, dims):
    return lax.dot_general(left, right, (dims, ((), ())), preferred_element_type=F32)


NN = ((1,), (0,))
NT = ((1,), (1,))
TN = ((0,), (0,))


def kernel(
    nz, dims, T,
    tok_ref, cot_ref, win_ref, wout_ref,
    out_ref, gtok_ref, gin_ref, gout_ref,
    own, tc, win, wout, part, zsend, zrecv, hid, osend, orecv,
    load_sem, gsend_sem, grecv_sem, zsend_sem, zrecv_sem, hsend_sem, hrecv_sem, osend_sem, orecv_sem,
):
    row, z = lax.axis_index("row"), lax.axis_index("col")
    X, Y, C = dims
    S = nz // 2

    def digits(i):
        return lax.div(i, Y * C), lax.rem(lax.div(i, C), Y), lax.rem(i, C)

    rx, ry, rc = digits(row)

    def plus(o):
        ox, oy, oc = digits(o)
        return (lax.rem(rx + ox, X) * Y + lax.rem(ry + oy, Y)) * C + lax.rem(rc + oc, C)

    def minus(o):
        ox, oy, oc = digits(o)
        return (lax.rem(rx - ox + X, X) * Y + lax.rem(ry - oy + Y, Y)) * C + lax.rem(rc - oc + C, C)

    def owner(p):
        half = lax.div(p + 1, 2)
        off = jnp.where(lax.rem(p, 2) == 0, S - half, half - S)
        return lax.rem(z + off + nz, nz)

    def rows(p, n=1):
        return pl.ds(pl.multiple_of(p * T, T), n * T)

    right, left = lax.rem(z + 1, nz), lax.rem(z + nz - 1, nz)
    side = (right, left)

    for i, (src, dst) in enumerate(
        ((tok_ref, own.at[0]), (cot_ref, own.at[1]), (win_ref, win), (wout_ref, wout))
    ):
        pltpu.make_async_copy(src, dst, load_sem.at[i]).start()

    barrier = pltpu.get_barrier_semaphore()
    for d in range(2):
        pl.semaphore_signal(barrier, inc=1, device_id=(row, side[d]), device_id_type=MESH)

    @pl.loop(1, nz)
    def _(o):
        pl.semaphore_signal(barrier, inc=1, device_id=(plus(o), z), device_id_type=MESH)

    for i, (src, dst) in enumerate(((tok_ref, own.at[0]), (cot_ref, own.at[1]))):
        pltpu.make_async_copy(src, dst, load_sem.at[i]).wait()
    pl.semaphore_wait(barrier, nz + 1)

    def gather(p, peer):
        return pltpu.make_async_remote_copy(
            src_ref=own, dst_ref=tc.at[:, rows(p)],
            send_sem=gsend_sem.at[p], recv_sem=grecv_sem.at[p],
            device_id=(peer, z), device_id_type=MESH,
        )

    def gather_self(p):
        return pltpu.make_async_copy(own, tc.at[:, rows(p)], grecv_sem.at[p])

    @pl.loop(0, nz)
    def _(p):
        o = owner(p)

        @pl.when(o != 0)
        def _():
            gather(p, minus(o)).start()

        @pl.when(o == 0)
        def _():
            gather_self(p).start()

    for i, (src, dst) in ((2, (win_ref, win)), (3, (wout_ref, wout))):
        pltpu.make_async_copy(src, dst, load_sem.at[i]).wait()

    def partials(lo, hi):
        @pl.loop(lo, hi)
        def _(p):
            gather_self(p).wait()

        r = slice(lo * T, hi * T)
        part[0, r, :] = mm(tc[0, r, :], win[...], NN)
        part[1, r, :] = mm(tc[1, r, :], wout[...], NT)

    def zcopy(d, i, s):
        return pltpu.make_async_remote_copy(
            src_ref=zsend.at[d, i, rows(s - 1)], dst_ref=zrecv.at[d, i, rows(s - 1)],
            send_sem=zsend_sem.at[d, i, s - 1], recv_sem=zrecv_sem.at[d, i, s - 1],
            device_id=(row, side[d]), device_id_type=MESH,
        )

    def zstep(s, both, first=False):
        for i in range(2):
            for d in range(both):
                value = part[i, rows(2 * (s - 1) + d), :]
                if not first:
                    zcopy(d, i, s - 1).wait_recv()
                    value = value + decode(zrecv[d, i, rows(s - 2), :])
                zsend[d, i, rows(s - 1), :] = encode(value)
                zcopy(d, i, s).start()

    bounds = sorted({b for b in (1, 2, 5, 9, 13) if b <= S} | {S + 1})
    groups = [(a, b) for a, b in zip(bounds[:-1], bounds[1:])]
    place = {}
    for a, b in groups[1:]:
        place.setdefault(max(1, a - 2), []).append((2 * (a - 1), 2 * (b - 1)))
    partials(0, 2 * (groups[0][1] - 1))
    zstep(1, 2 if S > 1 else 1, True)
    done = 1
    for at in sorted(place):
        if at > done:
            pl.loop(done + 1, at + 1)(lambda s: zstep(s, 2))
            done = at
        for g in place[at]:
            partials(*g)
    if S - 1 > done:
        pl.loop(done + 1, S)(lambda s: zstep(s, 2))
    if S > 1:
        zstep(S, 1)

    def hslot(d, s):
        return nz - 2 * s - (1 - d)

    def hmove(d, i, s):
        src = nz - 1 if isinstance(s, int) and s == 1 else hslot(d, s - 1)
        return pltpu.make_async_remote_copy(
            src_ref=hid.at[i, rows(src)], dst_ref=hid.at[i, rows(hslot(d, s))],
            send_sem=hsend_sem.at[d, i, s - 1], recv_sem=hrecv_sem.at[d, i, s - 1],
            device_id=(row, side[d]), device_id_type=MESH,
        )

    own_rows = rows(nz - 1)
    slope = None
    for i in range(2):
        value = part[i, own_rows, :]
        for d, s in ((0, S), (1, S - 1)):
            if s >= 1:
                zcopy(d, i, s).wait_recv()
                value = value + decode(zrecv[d, i, rows(s - 1), :])
        if i == 0:
            value, slope = gelu_both(value)
        else:
            value = value * slope
        hid[i, own_rows, :] = value.astype(BF)
        for d in ((1, 0) if S > 1 else (1,)):
            hmove(d, i, 1).start()

    def ocopy(p, peer):
        return pltpu.make_async_remote_copy(
            src_ref=osend.at[:, rows(p)], dst_ref=orecv.at[:, rows(p)],
            send_sem=osend_sem.at[p], recv_sem=orecv_sem.at[p],
            device_id=(peer, z), device_id_type=MESH,
        )

    def ocopy_self(p):
        return pltpu.make_async_copy(osend.at[:, rows(p)], orecv.at[:, rows(p)], orecv_sem.at[p])

    def products(lo, hi):
        r = slice(lo * T, hi * T)
        osend[0, r, :] = mm(hid[0, r, :], wout[...], NN).astype(BF)
        osend[1, r, :] = mm(hid[1, r, :], win[...], NT).astype(BF)

        @pl.loop(lo, hi)
        def _(j):
            p = lo + hi - 1 - j
            o = owner(p)

            @pl.when(o != 0)
            def _():
                ocopy(p, plus(o)).start()

            @pl.when(o == 0)
            def _():
                ocopy_self(p).start()

    W = 128
    pieces = [(0, k) for k in range(gout_ref.shape[0] // W)] + [(1, k) for k in range(gin_ref.shape[0] // W)]
    half = nz // 2 * T

    def grad_piece(piece, r, add):
        which, k = piece
        c = slice(k * W, (k + 1) * W)
        if which == 0:
            ref, value = gout_ref, mm(hid[0, r, c], tc[1, r, :], TN)
        else:
            ref, value = gin_ref, mm(tc[0, r, c], hid[1, r, :], TN)
        ref[c, :] = ref[c, :] + value if add else value

    ends = sorted({e for e in (3, 7, 11, 14, 15) if e < S} | {S})
    top = nz
    waiting = list(pieces)
    for s in range(1, S + 1):
        for i in range(2):
            for d in ((1, 0) if s < S else (1,)):
                hmove(d, i, s).wait_recv()
                if s + (1 - d) < S:
                    hmove(d, i, s + 1).start()
        if s in ends:
            low = nz - 1 - 2 * s if s < S else 0
            products(low, top)
            top = low
        if 2 * s >= S + 1 and s < S and waiting:
            grad_piece(waiting.pop(0), slice(half, 2 * half), False)
    for piece in waiting:
        grad_piece(piece, slice(half, 2 * half), False)
    for piece in pieces:
        grad_piece(piece, slice(0, half), True)

    for p in range(nz):
        ocopy_self(p).wait()
    for i, (mine, ref) in enumerate(((own, out_ref), (own, gtok_ref))):
        total = own[i].astype(F32)
        for p in range(nz):
            total = total + orecv[i, rows(p), :].astype(F32)
        ref[...] = total.astype(BF)

    @pl.loop(0, nz)
    def _(p):
        @pl.when(owner(p) != 0)
        def _():
            gather(p, row).wait_send()
            ocopy(p, row).wait_send()

    for i in range(2):
        for d in range(2):
            @pl.loop(1, S + 1 - d)
            def _(s):
                zcopy(d, i, s).wait_send()

            @pl.loop(1, S + d)
            def _(s):
                pltpu.make_async_remote_copy(
                    src_ref=hid.at[i, rows(0)], dst_ref=hid.at[i, rows(0)],
                    send_sem=hsend_sem.at[d, i, s - 1], recv_sem=hrecv_sem.at[d, i, s - 1],
                    device_id=(row, side[d]), device_id_type=MESH,
                ).wait_send()


def on_device(nz, dims, tokens, w_in, w_out, cotangent):
    T, DL = tokens.shape
    HL = w_in.shape[1]
    S = nz // 2
    any_space = pl.BlockSpec(memory_space=pl.ANY)
    vmem = pl.BlockSpec(memory_space=pltpu.VMEM)
    dma = pltpu.SemaphoreType.DMA
    flops = 2 * 6 * nz * T * DL * HL
    return pl.pallas_call(
        functools.partial(kernel, nz, dims, T),
        out_shape=(
            jax.ShapeDtypeStruct((T, DL), BF),
            jax.ShapeDtypeStruct((T, DL), BF),
            jax.ShapeDtypeStruct((DL, HL), F32),
            jax.ShapeDtypeStruct((HL, DL), F32),
        ),
        in_specs=[any_space] * 4,
        out_specs=(vmem,) * 4,
        scratch_shapes=[
            pltpu.VMEM((2, T, DL), BF),
            pltpu.VMEM((2, nz * T, DL), BF),
            pltpu.VMEM((DL, HL), BF),
            pltpu.VMEM((HL, DL), BF),
            pltpu.VMEM((2, nz * T, HL), F32),
            pltpu.VMEM((2, 2, S * T, HL), BF),
            pltpu.VMEM((2, 2, S * T, HL), BF),
            pltpu.VMEM((2, nz * T, HL), BF),
            pltpu.VMEM((2, nz * T, DL), BF),
            pltpu.VMEM((2, nz * T, DL), BF),
            dma((4,)),
            dma((nz,)),
            dma((nz,)),
            dma((2, 2, S)),
            dma((2, 2, S)),
            dma((2, 2, S)),
            dma((2, 2, S)),
            dma((nz,)),
            dma((nz,)),
        ],
        compiler_params=pltpu.CompilerParams(
            collective_id=0, has_side_effects=True, vmem_limit_bytes=40 * 2**20
        ),
        cost_estimate=pl.CostEstimate(flops=flops, bytes_accessed=4 * DL * HL * 3, transcendentals=0),
    )(tokens, cotangent, w_in, w_out)


def solution(mesh):
    nz = mesh.shape["col"]
    dims = {32: (4, 4, 2), 8: (2, 2, 2), 4: (1, 2, 2)}[mesh.shape["row"]]
    return jax.shard_map(
        functools.partial(on_device, nz, dims),
        mesh=mesh,
        in_specs=(P("row", "col"), P("col", "row"), P("row", "col"), P("row", "col")),
        out_specs=(P("row", "col"), P("row", "col"), P("col", "row"), P("row", "col")),
        check_vma=False,
    )
```

```python
import functools

import jax
import jax.numpy as jnp
from jax import lax
from jax.experimental import pallas as pl
from jax.experimental.pallas import tpu as pltpu
from jax.sharding import PartitionSpec as P

slope_c = 0.7978845608028654
cubic_k = 0.044715
MESH = pl.DeviceIdType.MESH
SCALE = 2.0**20
BF = jnp.bfloat16
F32 = jnp.float32


def gelu_both(h):
    tval = jnp.tanh(slope_c * (h + cubic_k * h * h * h))
    value = 0.5 * h * (1.0 + tval)
    slope = 0.5 * (1.0 + tval) + 0.5 * h * (1.0 - tval * tval) * slope_c * (
        1.0 + 3.0 * cubic_k * h * h
    )
    return value, slope


def encode(x):
    a = x * SCALE
    a = a * a
    a = a * a
    return jnp.where(x < 0.0, -a, a).astype(BF)


def decode(y):
    y = y.astype(F32)
    a = jnp.sqrt(jnp.sqrt(jnp.abs(y))) * (1.0 / SCALE)
    return jnp.where(y < 0.0, -a, a)


def mm(left, right, dims):
    return lax.dot_general(left, right, (dims, ((), ())), preferred_element_type=F32)


NN = ((1,), (0,))
NT = ((1,), (1,))
TN = ((0,), (0,))


def kernel(
    nz, dims, T,
    tok_ref, cot_ref, win_ref, wout_ref,
    out_ref, gtok_ref, gin_ref, gout_ref,
    own, tc, win, wout, part, zsend, zrecv, hid, osend, orecv, gin, gout, ends,
    load_sem, gsend_sem, grecv_sem, zsend_sem, zrecv_sem, hsend_sem, hrecv_sem, osend_sem, orecv_sem, store_sem,
):
    row, z = lax.axis_index("row"), lax.axis_index("col")
    X, Y, C = dims
    S = nz // 2
    J = S // 2

    def digits(i):
        return lax.div(i, Y * C), lax.rem(lax.div(i, C), Y), lax.rem(i, C)

    rx, ry, rc = digits(row)

    def plus(o):
        ox, oy, oc = digits(o)
        return (lax.rem(rx + ox, X) * Y + lax.rem(ry + oy, Y)) * C + lax.rem(rc + oc, C)

    def minus(o):
        ox, oy, oc = digits(o)
        return (lax.rem(rx - ox + X, X) * Y + lax.rem(ry - oy + Y, Y)) * C + lax.rem(rc - oc + C, C)

    def owner(p):
        half = lax.div(p + 1, 2)
        off = jnp.where(lax.rem(p, 2) == 0, S - half, half - S)
        return lax.rem(z + off + nz, nz)

    def rows(p, n=1):
        return pl.ds(pl.multiple_of(p * T, T), n * T)

    side = (lax.rem(z + 1, nz), lax.rem(z + nz - 1, nz))
    far = (lax.rem(z + 2, nz), lax.rem(z + nz - 2, nz))
    ring = side + (far if nz > 4 else far[:1])

    for i, (src, dst) in enumerate(
        ((tok_ref, own.at[0]), (cot_ref, own.at[1]), (win_ref, win), (wout_ref, wout))
    ):
        pltpu.make_async_copy(src, dst, load_sem.at[i]).start()

    barrier = pltpu.get_barrier_semaphore()
    for peer in ring:
        pl.semaphore_signal(barrier, inc=1, device_id=(row, peer), device_id_type=MESH)

    @pl.loop(1, nz)
    def _(o):
        pl.semaphore_signal(barrier, inc=1, device_id=(plus(o), z), device_id_type=MESH)

    for i, (src, dst) in enumerate(((tok_ref, own.at[0]), (cot_ref, own.at[1]))):
        pltpu.make_async_copy(src, dst, load_sem.at[i]).wait()
    pl.semaphore_wait(barrier, nz - 1 + len(ring))

    def gather(p, peer):
        return pltpu.make_async_remote_copy(
            src_ref=own, dst_ref=tc.at[:, rows(p)],
            send_sem=gsend_sem.at[p], recv_sem=grecv_sem.at[p],
            device_id=(peer, z), device_id_type=MESH,
        )

    def gather_self(p):
        return pltpu.make_async_copy(own, tc.at[:, rows(p)], grecv_sem.at[p])

    @pl.loop(0, nz)
    def _(p):
        o = owner(p)

        @pl.when(o != 0)
        def _():
            gather(p, minus(o)).start()

        @pl.when(o == 0)
        def _():
            gather_self(p).start()

    for i, (src, dst) in ((2, (win_ref, win)), (3, (wout_ref, wout))):
        pltpu.make_async_copy(src, dst, load_sem.at[i]).wait()

    def partials(lo, hi):
        @pl.loop(lo, hi)
        def _(p):
            gather_self(p).wait()

        r = slice(lo * T, hi * T)
        part[0, r, :] = mm(tc[0, r, :], win[...], NN)
        part[1, r, :] = mm(tc[1, r, :], wout[...], NT)

    def zcopy(d, i, slot, peer):
        return pltpu.make_async_remote_copy(
            src_ref=zsend.at[d, i, rows(slot)], dst_ref=zrecv.at[d, i, rows(slot)],
            send_sem=zsend_sem.at[d, i, slot], recv_sem=zrecv_sem.at[d, i, slot],
            device_id=(row, peer[d]), device_id_type=MESH,
        )

    def arrived(d, i, slot):
        zcopy(d, i, slot, side).wait_recv()
        return decode(zrecv[d, i, rows(slot), :])

    def zstep(j, first):
        for i in range(2):
            for d in range(2):
                if first == 0 and d == 1:
                    continue
                value = part[i, rows(4 * j - d), :]
                if first > 0:
                    value = value + arrived(d, i, J + j - 1)
                if first > d:
                    value = value + arrived(d, i, j - 1)
                zsend[d, i, rows(j), :] = encode(value)
                zcopy(d, i, j, far).start()
        for i in range(2):
            for d in range(2):
                zsend[d, i, rows(J + j), :] = encode(part[i, rows(4 * j + 2 - d), :])
                zcopy(d, i, J + j, side).start()

    partials(0, 4)
    zstep(0, 0)
    done = 0
    for lo, hi in ((4, 8), (8, 16), (16, nz)):
        if hi <= nz and lo < hi:
            partials(lo, hi)
            if done + 1 < J:
                done += 1
                zstep(done, min(done, 2))
    if done + 1 < J:
        pl.loop(done + 1, J)(lambda j: zstep(j, 2))

    def hslot(d, k):
        return 2 * (S - k) - 1 + (d if k else 0)

    def hfar(d, i, j):
        return pltpu.make_async_remote_copy(
            src_ref=hid.at[i, rows(hslot(d, 2 * j))], dst_ref=hid.at[i, rows(hslot(d, 2 * j + 2))],
            send_sem=hsend_sem.at[d, i, j], recv_sem=hrecv_sem.at[d, i, j],
            device_id=(row, far[d]), device_id_type=MESH,
        )

    def hnear(d, i, j):
        return pltpu.make_async_remote_copy(
            src_ref=hid.at[i, rows(hslot(d, 2 * j))], dst_ref=hid.at[i, rows(hslot(d, 2 * j + 1))],
            send_sem=hsend_sem.at[d, i, J + j], recv_sem=hrecv_sem.at[d, i, J + j],
            device_id=(row, side[d]), device_id_type=MESH,
        )

    def last(d):
        return J - 1 + d

    def forward(i, j):
        for d in (1, 0):
            if j > 0 and j <= last(d):
                hfar(d, i, j - 1).wait_recv()
            if j < last(d):
                hfar(d, i, j).start()
            if j < J:
                hnear(d, i, j).start()

    own_rows = rows(nz - 1)
    slope = None
    for i in range(2):
        value = part[i, own_rows, :]
        for d in range(2):
            value = value + arrived(d, i, 2 * J - 1)
            if J - 1 >= d:
                value = value + arrived(d, i, J - 1)
        if i == 0:
            value, slope = gelu_both(value)
        else:
            value = value * slope
        hid[i, own_rows, :] = value.astype(BF)
        forward(i, 0)

    def ocopy(p, peer):
        return pltpu.make_async_remote_copy(
            src_ref=osend.at[:, rows(p)], dst_ref=orecv.at[:, rows(p)],
            send_sem=osend_sem.at[p], recv_sem=orecv_sem.at[p],
            device_id=(peer, z), device_id_type=MESH,
        )

    def ocopy_self(p):
        return pltpu.make_async_copy(osend.at[:, rows(p)], orecv.at[:, rows(p)], orecv_sem.at[p])

    def products(lo, hi):
        r = slice(lo * T, hi * T)
        osend[0, r, :] = mm(hid[0, r, :], wout[...], NN).astype(BF)
        osend[1, r, :] = mm(hid[1, r, :], win[...], NT).astype(BF)

        @pl.loop(lo, hi)
        def _(j):
            p = lo + hi - 1 - j
            o = owner(p)

            @pl.when(o != 0)
            def _():
                ocopy(p, plus(o)).start()

            @pl.when(o == 0)
            def _():
                ocopy_self(p).start()

    W = 128
    pieces = [(0, k) for k in range(gout_ref.shape[0] // W)] + [(1, k) for k in range(gin_ref.shape[0] // W)]
    half = nz // 2 * T

    def grad_piece(piece, r, add):
        which, k = piece
        c = slice(k * W, (k + 1) * W)
        if which == 0:
            ref, value = gout, mm(hid[0, r, c], tc[1, r, :], TN)
        else:
            ref, value = gin, mm(tc[0, r, c], hid[1, r, :], TN)
        ref[c, :] = ref[c, :] + value if add else value

    stops = sorted({e for e in (2, 4, 6, 7) if e < J} | {J})
    top = nz
    waiting = list(pieces)
    near = 0
    for j in range(1, J + 1):
        for i in range(2):
            forward(i, j)
        if j in stops:
            for n in range(near, j):
                for i in range(2):
                    for d in range(2):
                        hnear(d, i, n).wait_recv()
            near = j
            low = nz - 1 - 4 * j if j < J else 0
            products(low, top)
            top = low
        if J // 2 < j < J:
            for piece in waiting[:3]:
                grad_piece(piece, slice(half, 2 * half), False)
            waiting = waiting[3:]
    for piece in waiting:
        grad_piece(piece, slice(half, 2 * half), False)
    stores = []

    def put(src, dst):
        stores.append(pltpu.make_async_copy(src, dst, store_sem.at[len(stores)]))
        stores[-1].start()

    for piece in pieces:
        grad_piece(piece, slice(0, half), True)
        c = slice(piece[1] * W, (piece[1] + 1) * W)
        if piece[0] == 0:
            put(gout.at[c], gout_ref.at[c])
        else:
            put(gin.at[c], gin_ref.at[c])

    for p in range(nz):
        ocopy_self(p).wait()
    for i, ref in enumerate((out_ref, gtok_ref)):
        total = own[i].astype(F32)
        for p in range(nz):
            total = total + orecv[i, rows(p), :].astype(F32)
        ends[i] = total.astype(BF)
        put(ends.at[i], ref)

    @pl.loop(0, nz)
    def _(p):
        @pl.when(owner(p) != 0)
        def _():
            gather(p, row).wait_send()
            ocopy(p, row).wait_send()

    for i in range(2):
        for d in range(2):
            @pl.loop(0, S)
            def _(slot):
                @pl.when(slot >= d)
                def _():
                    zcopy(d, i, slot, side).wait_send()

            for j in range(J):
                hnear(d, i, j).wait_send()
                if j < last(d):
                    hfar(d, i, j).wait_send()
    for copy in stores:
        copy.wait()


def store(*refs):
    copies = [pltpu.make_async_copy(refs[i], refs[4 + i], refs[8].at[i]) for i in range(4)]
    for copy in copies:
        copy.start()
    for copy in copies:
        copy.wait()


def on_device(nz, dims, tokens, w_in, w_out, cotangent):
    T, DL = tokens.shape
    HL = w_in.shape[1]
    S = nz // 2
    hbm = pl.BlockSpec(memory_space=pltpu.HBM)
    dma = pltpu.SemaphoreType.DMA
    flops = 2 * 6 * nz * T * DL * HL
    outs = (
        jax.ShapeDtypeStruct((T, DL), BF),
        jax.ShapeDtypeStruct((T, DL), BF),
        jax.ShapeDtypeStruct((DL, HL), F32),
        jax.ShapeDtypeStruct((HL, DL), F32),
    )
    results = pl.pallas_call(
        functools.partial(kernel, nz, dims, T),
        out_shape=outs,
        in_specs=[hbm] * 4,
        out_specs=(hbm,) * 4,
        scratch_shapes=[
            pltpu.VMEM((2, T, DL), BF),
            pltpu.VMEM((2, nz * T, DL), BF),
            pltpu.VMEM((DL, HL), BF),
            pltpu.VMEM((HL, DL), BF),
            pltpu.VMEM((2, nz * T, HL), F32),
            pltpu.VMEM((2, 2, S * T, HL), BF),
            pltpu.VMEM((2, 2, S * T, HL), BF),
            pltpu.VMEM((2, nz * T, HL), BF),
            pltpu.VMEM((2, nz * T, DL), BF),
            pltpu.VMEM((2, nz * T, DL), BF),
            pltpu.VMEM((DL, HL), F32),
            pltpu.VMEM((HL, DL), F32),
            pltpu.VMEM((2, T, DL), BF),
            dma((4,)),
            dma((nz,)),
            dma((nz,)),
            dma((2, 2, S)),
            dma((2, 2, S)),
            dma((2, 2, S)),
            dma((2, 2, S)),
            dma((nz,)),
            dma((nz,)),
            dma((2 + (DL + HL) // 128,)),
        ],
        compiler_params=pltpu.CompilerParams(
            collective_id=0, has_side_effects=True, vmem_limit_bytes=58 * 2**20
        ),
        cost_estimate=pl.CostEstimate(flops=flops, bytes_accessed=4 * DL * HL * 3, transcendentals=0),
    )(tokens, cotangent, w_in, w_out)
    return pl.pallas_call(
        store,
        out_shape=outs,
        in_specs=[pl.BlockSpec(memory_space=pl.ANY)] * 4,
        out_specs=(hbm,) * 4,
        scratch_shapes=[dma((4,))],
        compiler_params=pltpu.CompilerParams(vmem_limit_bytes=58 * 2**20),
    )(*results)


def solution(mesh):
    nz = mesh.shape["col"]
    dims = {32: (4, 4, 2), 8: (2, 2, 2), 4: (1, 2, 2)}[mesh.shape["row"]]
    return jax.shard_map(
        functools.partial(on_device, nz, dims),
        mesh=mesh,
        in_specs=(P("row", "col"), P("col", "row"), P("row", "col"), P("row", "col")),
        out_specs=(P("row", "col"), P("row", "col"), P("col", "row"), P("row", "col")),
        check_vma=False,
    )
```

```python
import functools

import jax
import jax.numpy as jnp
from jax import lax
from jax.experimental import pallas as pl
from jax.experimental.pallas import tpu as pltpu
from jax.sharding import PartitionSpec as P

slope_c = 0.7978845608028654
cubic_k = 0.044715
MESH = pl.DeviceIdType.MESH
SCALE = 2.0**20
BF = jnp.bfloat16
F32 = jnp.float32


def gelu_both(h):
    tval = jnp.tanh(slope_c * (h + cubic_k * h * h * h))
    value = 0.5 * h * (1.0 + tval)
    slope = 0.5 * (1.0 + tval) + 0.5 * h * (1.0 - tval * tval) * slope_c * (
        1.0 + 3.0 * cubic_k * h * h
    )
    return value, slope


def encode(x):
    a = x * SCALE
    a = a * a
    a = a * a
    return jnp.where(x < 0.0, -a, a).astype(BF)


def decode(y):
    y = y.astype(F32)
    a = jnp.sqrt(jnp.sqrt(jnp.abs(y))) * (1.0 / SCALE)
    return jnp.where(y < 0.0, -a, a)


def mm(left, right, dims):
    return lax.dot_general(left, right, (dims, ((), ())), preferred_element_type=F32)


NN = ((1,), (0,))
NT = ((1,), (1,))
TN = ((0,), (0,))


def kernel(
    nz, T,
    tok_ref, cot_ref, win_ref, wout_ref,
    out_ref, gtok_ref, gin_ref, gout_ref,
    own, tc, win, wout, part, zsend, zrecv, hid, osend, orecv, gin, gout, ends,
    load_sem, gsend_sem, grecv_sem, zsend_sem, zrecv_sem, hsend_sem, hrecv_sem, osend_sem, orecv_sem, store_sem,
):
    row, z = lax.axis_index("row"), lax.axis_index("col")
    S = nz // 2
    J = S // 2

    def plus(o):
        return lax.rem(row + o, nz)

    def minus(o):
        return lax.rem(row - o + nz, nz)

    def owner(p):
        half = lax.div(p + 1, 2)
        off = jnp.where(lax.rem(p, 2) == 0, S - half, half - S)
        return lax.rem(z + off + nz, nz)

    def rows(p, n=1):
        return pl.ds(pl.multiple_of(p * T, T), n * T)

    side = (lax.rem(z + 1, nz), lax.rem(z + nz - 1, nz))
    far = (lax.rem(z + 2, nz), lax.rem(z + nz - 2, nz))
    ring = side + (far if nz > 4 else far[:1])

    for i, (src, dst) in enumerate(
        ((tok_ref, own.at[0]), (cot_ref, own.at[1]), (win_ref, win), (wout_ref, wout))
    ):
        pltpu.make_async_copy(src, dst, load_sem.at[i]).start()

    barrier = pltpu.get_barrier_semaphore()
    for peer in ring:
        pl.semaphore_signal(barrier, inc=1, device_id=(row, peer), device_id_type=MESH)

    @pl.loop(1, nz)
    def _(o):
        pl.semaphore_signal(barrier, inc=1, device_id=(plus(o), z), device_id_type=MESH)

    for i, (src, dst) in enumerate(((tok_ref, own.at[0]), (cot_ref, own.at[1]))):
        pltpu.make_async_copy(src, dst, load_sem.at[i]).wait()
    pl.semaphore_wait(barrier, nz - 1 + len(ring))

    def gather(p, peer):
        return pltpu.make_async_remote_copy(
            src_ref=own, dst_ref=tc.at[:, rows(p)],
            send_sem=gsend_sem.at[p], recv_sem=grecv_sem.at[p],
            device_id=(peer, z), device_id_type=MESH,
        )

    def gather_self(p):
        return pltpu.make_async_copy(own, tc.at[:, rows(p)], grecv_sem.at[p])

    def spread(lo, hi):
        @pl.loop(lo, hi)
        def _(p):
            o = owner(p)

            @pl.when(o != 0)
            def _():
                gather(p, minus(o)).start()

            @pl.when(o == 0)
            def _():
                gather_self(p).start()

    spread(0, min(8, nz))

    for i, (src, dst) in ((2, (win_ref, win)), (3, (wout_ref, wout))):
        pltpu.make_async_copy(src, dst, load_sem.at[i]).wait()

    def partials(lo, hi):
        @pl.loop(lo, hi)
        def _(p):
            gather_self(p).wait()

        r = slice(lo * T, hi * T)
        part[0, r, :] = mm(tc[0, r, :], win[...], NN)
        part[1, r, :] = mm(tc[1, r, :], wout[...], NT)

    def zcopy(d, i, slot, peer):
        return pltpu.make_async_remote_copy(
            src_ref=zsend.at[d, i, rows(slot)], dst_ref=zrecv.at[d, i, rows(slot)],
            send_sem=zsend_sem.at[d, i, slot], recv_sem=zrecv_sem.at[d, i, slot],
            device_id=(row, peer[d]), device_id_type=MESH,
        )

    def arrived(d, i, slot):
        zcopy(d, i, slot, side).wait_recv()
        return decode(zrecv[d, i, rows(slot), :])

    def zfar(j, first):
        for i in range(2):
            for d in range(2):
                if first == 0 and d == 1:
                    continue
                value = part[i, rows(4 * j - d), :]
                if first > 0:
                    value = value + arrived(d, i, J + j - 1)
                if first > d:
                    value = value + arrived(d, i, j - 1)
                zsend[d, i, rows(j), :] = encode(value)
                zcopy(d, i, j, far).start()

    def znear(j):
        for i in range(2):
            for d in range(2):
                zsend[d, i, rows(J + j), :] = encode(part[i, rows(4 * j + 2 - d), :])
                zcopy(d, i, J + j, side).start()

    def zstep(j, first):
        znear(j)
        zfar(j, first)

    partials(0, 4)
    zfar(0, 0)
    znear(0)
    if J > 1:
        if nz > 8:
            spread(8, 16)
        partials(4, 8)
        zstep(1, 1)
    if J > 2:
        if nz > 16:
            spread(16, nz)
        partials(8, 16)
        zstep(2, 2)
        zstep(3, 2)
    if J > 4:
        partials(16, nz)
        pl.loop(4, J)(lambda j: zstep(j, 2))

    def hslot(d, k):
        return 2 * (S - k) - 1 + (d if k else 0)

    def hfar(d, i, j):
        return pltpu.make_async_remote_copy(
            src_ref=hid.at[i, rows(hslot(d, 2 * j))], dst_ref=hid.at[i, rows(hslot(d, 2 * j + 2))],
            send_sem=hsend_sem.at[d, i, j], recv_sem=hrecv_sem.at[d, i, j],
            device_id=(row, far[d]), device_id_type=MESH,
        )

    def hnear(d, i, j):
        return pltpu.make_async_remote_copy(
            src_ref=hid.at[i, rows(hslot(d, 2 * j))], dst_ref=hid.at[i, rows(hslot(d, 2 * j + 1))],
            send_sem=hsend_sem.at[d, i, J + j], recv_sem=hrecv_sem.at[d, i, J + j],
            device_id=(row, side[d]), device_id_type=MESH,
        )

    def last(d):
        return J - 1 + d

    def forward(i, j):
        for d in (1, 0):
            if j > 0 and j <= last(d):
                hfar(d, i, j - 1).wait_recv()
            if j < last(d):
                hfar(d, i, j).start()
            if j < J:
                hnear(d, i, j).start()

    own_rows = rows(nz - 1)
    slope = None
    for i in range(2):
        value = part[i, own_rows, :]
        for d in range(2):
            value = value + arrived(d, i, 2 * J - 1)
            if J - 1 >= d:
                value = value + arrived(d, i, J - 1)
        if i == 0:
            value, slope = gelu_both(value)
        else:
            value = value * slope
        hid[i, own_rows, :] = value.astype(BF)
        forward(i, 0)

    def ocopy(p, peer):
        return pltpu.make_async_remote_copy(
            src_ref=osend.at[:, rows(p)], dst_ref=orecv.at[:, rows(p)],
            send_sem=osend_sem.at[p], recv_sem=orecv_sem.at[p],
            device_id=(peer, z), device_id_type=MESH,
        )

    def ocopy_self(p):
        return pltpu.make_async_copy(osend.at[:, rows(p)], orecv.at[:, rows(p)], orecv_sem.at[p])

    def products(lo, hi):
        r = slice(lo * T, hi * T)
        osend[0, r, :] = mm(hid[0, r, :], wout[...], NN).astype(BF)
        osend[1, r, :] = mm(hid[1, r, :], win[...], NT).astype(BF)

        @pl.loop(lo, hi)
        def _(j):
            p = lo + hi - 1 - j
            o = owner(p)

            @pl.when(o != 0)
            def _():
                ocopy(p, plus(o)).start()

            @pl.when(o == 0)
            def _():
                ocopy_self(p).start()

    W = 128
    pieces = [(0, k) for k in range(gout_ref.shape[0] // W)] + [(1, k) for k in range(gin_ref.shape[0] // W)]
    half = nz // 2 * T

    def grad_piece(piece, r, add):
        which, k = piece
        c = slice(k * W, (k + 1) * W)
        if which == 0:
            ref, value = gout, mm(hid[0, r, c], tc[1, r, :], TN)
        else:
            ref, value = gin, mm(tc[0, r, c], hid[1, r, :], TN)
        ref[c, :] = ref[c, :] + value if add else value

    top = nz
    waiting = list(pieces)
    near = 0

    def ready(n):
        nonlocal near
        for k in range(near, n):
            for i in range(2):
                for d in range(2):
                    hnear(d, i, k).wait_recv()
        near = n

    def multiply(low):
        nonlocal top
        if low < top:
            products(low, top)
            top = low

    for j in range(1, J + 1):
        for i in range(2):
            forward(i, j)
        if j % 2 == 1 and j >= 3 or j == J:
            ready(j - 1)
            multiply(nz - 1 - 4 * (j - 1))
        if top <= nz // 2 and j < J:
            for piece in waiting[:3]:
                grad_piece(piece, slice(half, 2 * half), False)
            waiting = waiting[3:]
    ready(J)
    multiply(0)
    for piece in waiting:
        grad_piece(piece, slice(half, 2 * half), False)

    stores = []

    def put(src, dst):
        stores.append(pltpu.make_async_copy(src, dst, store_sem.at[len(stores)]))
        stores[-1].start()

    for piece in pieces:
        grad_piece(piece, slice(0, half), True)
        c = slice(piece[1] * W, (piece[1] + 1) * W)
        if piece[0] == 0:
            put(gout.at[c], gout_ref.at[c])
        else:
            put(gin.at[c], gin_ref.at[c])

    for p in range(nz):
        ocopy_self(p).wait()
    for i, ref in enumerate((out_ref, gtok_ref)):
        total = own[i].astype(F32)
        for p in range(nz):
            total = total + orecv[i, rows(p), :].astype(F32)
        ends[i] = total.astype(BF)
        put(ends.at[i], ref)

    @pl.loop(0, nz)
    def _(p):
        @pl.when(owner(p) != 0)
        def _():
            gather(p, row).wait_send()
            ocopy(p, row).wait_send()

    for i in range(2):
        for d in range(2):
            @pl.loop(0, S)
            def _(slot):
                @pl.when(slot >= d)
                def _():
                    zcopy(d, i, slot, side).wait_send()

            for j in range(J):
                hnear(d, i, j).wait_send()
                if j < last(d):
                    hfar(d, i, j).wait_send()
    for copy in stores:
        copy.wait()


def store(*refs):
    sources, targets, held, sems = refs[:4], refs[4:8], refs[8:12], refs[12]
    moves = []
    for source, target, block in zip(sources, targets, held):
        height = min(128, source.shape[0])
        for top in range(0, source.shape[0], height):
            c, n = pl.ds(top, height), len(moves)
            moves.append(
                (
                    pltpu.make_async_copy(source.at[c], block.at[c], sems.at[0, n]),
                    pltpu.make_async_copy(block.at[c], target.at[c], sems.at[1, n]),
                )
            )
    for load, _ in moves:
        load.start()
    for load, save in moves:
        load.wait()
        save.start()
    for _, save in moves:
        save.wait()


def on_device(nz, tokens, w_in, w_out, cotangent):
    T, DL = tokens.shape
    HL = w_in.shape[1]
    S = nz // 2
    hbm = pl.BlockSpec(memory_space=pltpu.HBM)
    dma = pltpu.SemaphoreType.DMA
    flops = 2 * 6 * nz * T * DL * HL
    outs = (
        jax.ShapeDtypeStruct((T, DL), BF),
        jax.ShapeDtypeStruct((T, DL), BF),
        jax.ShapeDtypeStruct((DL, HL), F32),
        jax.ShapeDtypeStruct((HL, DL), F32),
    )
    results = pl.pallas_call(
        functools.partial(kernel, nz, T),
        out_shape=outs,
        in_specs=[hbm] * 4,
        out_specs=(hbm,) * 4,
        scratch_shapes=[
            pltpu.VMEM((2, T, DL), BF),
            pltpu.VMEM((2, nz * T, DL), BF),
            pltpu.VMEM((DL, HL), BF),
            pltpu.VMEM((HL, DL), BF),
            pltpu.VMEM((2, nz * T, HL), F32),
            pltpu.VMEM((2, 2, S * T, HL), BF),
            pltpu.VMEM((2, 2, S * T, HL), BF),
            pltpu.VMEM((2, nz * T, HL), BF),
            pltpu.VMEM((2, nz * T, DL), BF),
            pltpu.VMEM((2, nz * T, DL), BF),
            pltpu.VMEM((DL, HL), F32),
            pltpu.VMEM((HL, DL), F32),
            pltpu.VMEM((2, T, DL), BF),
            dma((4,)),
            dma((nz,)),
            dma((nz,)),
            dma((2, 2, S)),
            dma((2, 2, S)),
            dma((2, 2, S)),
            dma((2, 2, S)),
            dma((nz,)),
            dma((nz,)),
            dma((2 + (DL + HL) // 128,)),
        ],
        compiler_params=pltpu.CompilerParams(
            collective_id=0, has_side_effects=True, vmem_limit_bytes=58 * 2**20
        ),
        cost_estimate=pl.CostEstimate(flops=flops, bytes_accessed=4 * DL * HL * 3, transcendentals=0),
    )(tokens, cotangent, w_in, w_out)
    return pl.pallas_call(
        store,
        out_shape=outs,
        in_specs=[pl.BlockSpec(memory_space=pl.ANY)] * 4,
        out_specs=(hbm,) * 4,
        scratch_shapes=[pltpu.VMEM(out.shape, out.dtype) for out in outs] + [dma((2, 2 + (DL + HL) // 128))],
        compiler_params=pltpu.CompilerParams(vmem_limit_bytes=58 * 2**20),
    )(*results)


def solution(mesh):
    nz = mesh.shape["col"]
    return jax.shard_map(
        functools.partial(on_device, nz),
        mesh=mesh,
        in_specs=(P("row", "col"), P("col", "row"), P("row", "col"), P("row", "col")),
        out_specs=(P("row", "col"), P("row", "col"), P("col", "row"), P("row", "col")),
        check_vma=False,
    )
```

```python
import functools

import jax
import jax.numpy as jnp
from jax import lax
from jax.experimental import pallas as pl
from jax.experimental.pallas import tpu as pltpu
from jax.sharding import PartitionSpec as P

slope_c = 0.7978845608028654
cubic_k = 0.044715
MESH = pl.DeviceIdType.MESH
SCALE = 2.0**20
BF = jnp.bfloat16
F32 = jnp.float32


def gelu_both(h):
    tval = jnp.tanh(slope_c * (h + cubic_k * h * h * h))
    value = 0.5 * h * (1.0 + tval)
    slope = 0.5 * (1.0 + tval) + 0.5 * h * (1.0 - tval * tval) * slope_c * (
        1.0 + 3.0 * cubic_k * h * h
    )
    return value, slope


def encode(x):
    a = x * SCALE
    a = a * a
    a = a * a
    return jnp.where(x < 0.0, -a, a).astype(BF)


def decode(y):
    y = y.astype(F32)
    a = jnp.sqrt(jnp.sqrt(jnp.abs(y))) * (1.0 / SCALE)
    return jnp.where(y < 0.0, -a, a)


def mm(left, right, dims):
    return lax.dot_general(left, right, (dims, ((), ())), preferred_element_type=F32)


NN = ((1,), (0,))
NT = ((1,), (1,))
TN = ((0,), (0,))


def kernel(
    nz, T,
    tok_ref, cot_ref, win_ref, wout_ref,
    out_ref, gtok_ref, gin_ref, gout_ref,
    own, tc, win, wout, part, zsend, zrecv, hid, osend, orecv, gin, gout, ends,
    load_sem, gsend_sem, grecv_sem, zsend_sem, zrecv_sem, hsend_sem, hrecv_sem, osend_sem, orecv_sem, store_sem,
):
    row, z = lax.axis_index("row"), lax.axis_index("col")
    S = nz // 2
    J = S // 2

    def wrap(v):
        return jnp.where(v >= nz, v - nz, v)

    def plus(o):
        return wrap(row + o)

    def minus(o):
        return wrap(row - o + nz)

    def owner(p):
        if isinstance(p, int):
            k = S - p // 2 if p % 2 == 0 else nz + (p + 1) // 2 - S
            return wrap(z + k % nz)
        half = lax.div(p + 1, 2)
        return wrap(z + jnp.where(lax.rem(p, 2) == 0, S - half, wrap(half - S + nz)))

    def rows(p, n=1):
        return pl.ds(pl.multiple_of(p * T, T), n * T)

    side = (wrap(z + 1), wrap(z + nz - 1))
    far = (wrap(z + 2), wrap(z + nz - 2))
    ring = side + (far if nz > 4 else far[:1])

    for i, (src, dst) in enumerate(
        ((tok_ref, own.at[0]), (cot_ref, own.at[1]), (win_ref, win), (wout_ref, wout))
    ):
        pltpu.make_async_copy(src, dst, load_sem.at[i]).start()

    barrier = pltpu.get_barrier_semaphore()
    for peer in ring:
        pl.semaphore_signal(barrier, inc=1, device_id=(row, peer), device_id_type=MESH)

    @pl.loop(1, nz)
    def _(o):
        pl.semaphore_signal(barrier, inc=1, device_id=(plus(o), z), device_id_type=MESH)

    for i, (src, dst) in enumerate(((tok_ref, own.at[0]), (cot_ref, own.at[1]))):
        pltpu.make_async_copy(src, dst, load_sem.at[i]).wait()
    pl.semaphore_wait(barrier, nz - 1 + len(ring))

    def gather(p, peer):
        return pltpu.make_async_remote_copy(
            src_ref=own, dst_ref=tc.at[:, rows(p)],
            send_sem=gsend_sem.at[p], recv_sem=grecv_sem.at[p],
            device_id=(peer, z), device_id_type=MESH,
        )

    def gather_self(p):
        return pltpu.make_async_copy(own, tc.at[:, rows(p)], grecv_sem.at[p])

    def spread(lo, n):
        for k in range(n):
            p = lo + k
            o = owner(p)

            @pl.when(o != 0)
            def _():
                gather(p, minus(o)).start()

            @pl.when(o == 0)
            def _():
                gather_self(p).start()

    spread(0, min(8, nz))
    for i, (src, dst) in ((2, (win_ref, win)), (3, (wout_ref, wout))):
        pltpu.make_async_copy(src, dst, load_sem.at[i]).wait()

    def partials(j):
        for k in range(4):
            gather_self(4 * j + k).wait()
        r = rows(4 * j, 4)
        part[0, r, :] = mm(tc[0, r, :], win[...], NN)
        part[1, r, :] = mm(tc[1, r, :], wout[...], NT)

    def zcopy(d, i, slot, peer):
        return pltpu.make_async_remote_copy(
            src_ref=zsend.at[d, i, rows(slot)], dst_ref=zrecv.at[d, i, rows(slot)],
            send_sem=zsend_sem.at[d, i, slot], recv_sem=zrecv_sem.at[d, i, slot],
            device_id=(row, peer[d]), device_id_type=MESH,
        )

    def arrived(d, i, slot):
        zcopy(d, i, slot, side).wait_recv()
        return decode(zrecv[d, i, rows(slot), :])

    def zfar(j, first):
        for i in range(2):
            for d in range(2):
                if first == 0 and d == 1:
                    continue
                value = part[i, rows(4 * j - d), :]
                if first > 0:
                    value = value + arrived(d, i, J + j - 1)
                if first > d:
                    value = value + arrived(d, i, j - 1)
                zsend[d, i, rows(j), :] = encode(value)
                zcopy(d, i, j, far).start()

    def znear(j):
        for i in range(2):
            for d in range(2):
                zsend[d, i, rows(J + j), :] = encode(part[i, rows(4 * j + 2 - d), :])
                zcopy(d, i, J + j, side).start()

    def zstep(j, first):
        partials(j)
        znear(j)
        zfar(j, first)

    partials(0)
    zfar(0, 0)
    znear(0)
    if J > 2:
        spread(8, 4)
    if J > 1:
        zstep(1, 1)
    if J > 2:
        if J > 3:
            spread(12, 4)

        @pl.loop(2, J)
        def _(j):
            @pl.when(j < J - 2)
            def _():
                spread(4 * j + 8, 4)

            zstep(j, 2)

    def hslot(d, k):
        return 2 * (S - k) - 1 + (d if k else 0)

    def hfar(d, i, j):
        return pltpu.make_async_remote_copy(
            src_ref=hid.at[i, rows(hslot(d, 2 * j))], dst_ref=hid.at[i, rows(hslot(d, 2 * j + 2))],
            send_sem=hsend_sem.at[d, i, j], recv_sem=hrecv_sem.at[d, i, j],
            device_id=(row, far[d]), device_id_type=MESH,
        )

    def hnear(d, i, j):
        return pltpu.make_async_remote_copy(
            src_ref=hid.at[i, rows(hslot(d, 2 * j))], dst_ref=hid.at[i, rows(hslot(d, 2 * j + 1))],
            send_sem=hsend_sem.at[d, i, J + j], recv_sem=hrecv_sem.at[d, i, J + j],
            device_id=(row, side[d]), device_id_type=MESH,
        )

    def last(d):
        return J - 1 + d

    def forward(i, j):
        for d in (1, 0):
            if j > 0 and j <= last(d):
                hfar(d, i, j - 1).wait_recv()
            if j < last(d):
                hfar(d, i, j).start()
            if j < J:
                hnear(d, i, j).start()

    own_rows = rows(nz - 1)
    slope = None
    for i in range(2):
        value = part[i, own_rows, :]
        for d in range(2):
            value = value + arrived(d, i, 2 * J - 1)
            if J - 1 >= d:
                value = value + arrived(d, i, J - 1)
        if i == 0:
            value, slope = gelu_both(value)
        else:
            value = value * slope
        hid[i, own_rows, :] = value.astype(BF)
        forward(i, 0)

    def ocopy(p, peer):
        return pltpu.make_async_remote_copy(
            src_ref=osend.at[:, rows(p)], dst_ref=orecv.at[:, rows(p)],
            send_sem=osend_sem.at[p], recv_sem=orecv_sem.at[p],
            device_id=(peer, z), device_id_type=MESH,
        )

    def ocopy_self(p):
        return pltpu.make_async_copy(osend.at[:, rows(p)], orecv.at[:, rows(p)], orecv_sem.at[p])

    def products(lo, hi):
        r = slice(lo * T, hi * T)
        osend[0, r, :] = mm(hid[0, r, :], wout[...], NN).astype(BF)
        osend[1, r, :] = mm(hid[1, r, :], win[...], NT).astype(BF)

        for p in reversed(range(lo, hi)):
            o = owner(p)

            @pl.when(o != 0)
            def _():
                ocopy(p, plus(o)).start()

            @pl.when(o == 0)
            def _():
                ocopy_self(p).start()

    W = 128
    pieces = [(0, k) for k in range(gout_ref.shape[0] // W)] + [(1, k) for k in range(gin_ref.shape[0] // W)]
    half = nz // 2 * T

    def grad_piece(piece, r, add):
        which, k = piece
        c = slice(k * W, (k + 1) * W)
        if which == 0:
            ref, value = gout, mm(hid[0, r, c], tc[1, r, :], TN)
        else:
            ref, value = gin, mm(tc[0, r, c], hid[1, r, :], TN)
        ref[c, :] = ref[c, :] + value if add else value

    top = nz
    waiting = list(pieces)
    near = 0

    def ready(n):
        nonlocal near
        for k in range(near, n):
            for i in range(2):
                for d in range(2):
                    hnear(d, i, k).wait_recv()
        near = n

    def multiply(low):
        nonlocal top
        if low < top:
            products(low, top)
            top = low

    def left(j):
        if j == 1:
            @pl.loop(0, nz)
            def _(p):
                @pl.when(owner(p) != 0)
                def _():
                    gather(p, row).wait_send()
        if 2 <= j <= 3 or J < 3 and j == J:
            for d in ((0, 1) if J < 3 else (j - 2,)):
                for i in range(2):
                    pl.loop(0, J)(lambda slot: zcopy(d, i, J + slot, side).wait_send())
                    pl.loop(d, J)(lambda slot: zcopy(d, i, slot, far).wait_send())

    def passed(j):
        for i in range(2):
            for d in range(2):
                if j < J:
                    hnear(d, i, j).wait_send()
                if j < last(d):
                    hfar(d, i, j).wait_send()

    for j in range(1, J + 1):
        for i in range(2):
            forward(i, j)
        if j > 1:
            ready(j - 1)
            multiply(nz - 1 - 4 * (j - 1))
        if top <= nz // 2 and j < J:
            for piece in waiting[:4]:
                grad_piece(piece, slice(half, 2 * half), False)
            waiting = waiting[4:]
        left(j)
        if j > 2:
            passed(j - 3)
    ready(J)
    multiply(0)
    for piece in waiting:
        grad_piece(piece, slice(half, 2 * half), False)

    stores = []

    def put(src, dst):
        stores.append(pltpu.make_async_copy(src, dst, store_sem.at[len(stores)]))
        stores[-1].start()

    for piece in pieces:
        grad_piece(piece, slice(0, half), True)
        c = slice(piece[1] * W, (piece[1] + 1) * W)
        if piece[0] == 0:
            put(gout.at[c], gout_ref.at[c])
        else:
            put(gin.at[c], gin_ref.at[c])

    for p in reversed(range(nz)):
        ocopy_self(p).wait()
    for i, ref in enumerate((out_ref, gtok_ref)):
        total = own[i].astype(F32)
        for p in range(nz):
            total = total + orecv[i, rows(p), :].astype(F32)
        ends[i] = total.astype(BF)
        put(ends.at[i], ref)

    for j in range(max(J - 2, 0), J):
        passed(j)

    @pl.loop(0, nz)
    def _(p):
        @pl.when(owner(p) != 0)
        def _():
            ocopy(p, row).wait_send()

    for copy in stores:
        copy.wait()


def store(*refs):
    sources, targets, held, sems = refs[:4], refs[4:8], refs[8:12], refs[12]
    moves = []
    for source, target, block in zip(sources, targets, held):
        height = min(128, source.shape[0])
        for top in range(0, source.shape[0], height):
            c, n = pl.ds(top, height), len(moves)
            moves.append(
                (
                    pltpu.make_async_copy(source.at[c], block.at[c], sems.at[0, n]),
                    pltpu.make_async_copy(block.at[c], target.at[c], sems.at[1, n]),
                )
            )
    for load, _ in moves:
        load.start()
    for load, save in moves:
        load.wait()
        save.start()
    for _, save in moves:
        save.wait()


def on_device(nz, tokens, w_in, w_out, cotangent):
    T, DL = tokens.shape
    HL = w_in.shape[1]
    S = nz // 2
    hbm = pl.BlockSpec(memory_space=pltpu.HBM)
    dma = pltpu.SemaphoreType.DMA
    flops = 2 * 6 * nz * T * DL * HL
    outs = (
        jax.ShapeDtypeStruct((T, DL), BF),
        jax.ShapeDtypeStruct((T, DL), BF),
        jax.ShapeDtypeStruct((DL, HL), F32),
        jax.ShapeDtypeStruct((HL, DL), F32),
    )
    results = pl.pallas_call(
        functools.partial(kernel, nz, T),
        out_shape=outs,
        in_specs=[hbm] * 4,
        out_specs=(hbm,) * 4,
        scratch_shapes=[
            pltpu.VMEM((2, T, DL), BF),
            pltpu.VMEM((2, nz * T, DL), BF),
            pltpu.VMEM((DL, HL), BF),
            pltpu.VMEM((HL, DL), BF),
            pltpu.VMEM((2, nz * T, HL), F32),
            pltpu.VMEM((2, 2, S * T, HL), BF),
            pltpu.VMEM((2, 2, S * T, HL), BF),
            pltpu.VMEM((2, nz * T, HL), BF),
            pltpu.VMEM((2, nz * T, DL), BF),
            pltpu.VMEM((2, nz * T, DL), BF),
            pltpu.VMEM((DL, HL), F32),
            pltpu.VMEM((HL, DL), F32),
            pltpu.VMEM((2, T, DL), BF),
            dma((4,)),
            dma((nz,)),
            dma((nz,)),
            dma((2, 2, S)),
            dma((2, 2, S)),
            dma((2, 2, S)),
            dma((2, 2, S)),
            dma((nz,)),
            dma((nz,)),
            dma((2 + (DL + HL) // 128,)),
        ],
        compiler_params=pltpu.CompilerParams(
            collective_id=0, has_side_effects=True, vmem_limit_bytes=58 * 2**20
        ),
        cost_estimate=pl.CostEstimate(flops=flops, bytes_accessed=4 * DL * HL * 3, transcendentals=0),
    )(tokens, cotangent, w_in, w_out)
    return pl.pallas_call(
        store,
        out_shape=outs,
        in_specs=[pl.BlockSpec(memory_space=pl.ANY)] * 4,
        out_specs=(hbm,) * 4,
        scratch_shapes=[pltpu.VMEM(out.shape, out.dtype) for out in outs] + [dma((2, 2 + (DL + HL) // 128))],
        compiler_params=pltpu.CompilerParams(vmem_limit_bytes=58 * 2**20),
    )(*results)


def solution(mesh):
    nz = mesh.shape["col"]
    return jax.shard_map(
        functools.partial(on_device, nz),
        mesh=mesh,
        in_specs=(P("row", "col"), P("col", "row"), P("row", "col"), P("row", "col")),
        out_specs=(P("row", "col"), P("row", "col"), P("col", "row"), P("row", "col")),
        check_vma=False,
    )
```

```python
import functools

import jax
import jax.numpy as jnp
from jax import lax
from jax.experimental import pallas as pl
from jax.experimental.pallas import tpu as pltpu
from jax.sharding import PartitionSpec as P

slope_c = 0.7978845608028654
cubic_k = 0.044715
MESH = pl.DeviceIdType.MESH
SCALE = 2.0**20
BF = jnp.bfloat16
F32 = jnp.float32


def gelu_both(h):
    tval = jnp.tanh(slope_c * (h + cubic_k * h * h * h))
    value = 0.5 * h * (1.0 + tval)
    slope = 0.5 * (1.0 + tval) + 0.5 * h * (1.0 - tval * tval) * slope_c * (
        1.0 + 3.0 * cubic_k * h * h
    )
    return value, slope


def encode(x):
    a = x * SCALE
    a = a * a
    a = a * a
    return jnp.where(x < 0.0, -a, a).astype(BF)


def decode(y):
    y = y.astype(F32)
    a = jnp.sqrt(jnp.sqrt(jnp.abs(y))) * (1.0 / SCALE)
    return jnp.where(y < 0.0, -a, a)


def mm(left, right, dims):
    return lax.dot_general(left, right, (dims, ((), ())), preferred_element_type=F32)


NN = ((1,), (0,))
NT = ((1,), (1,))
TN = ((0,), (0,))


def kernel(
    nz, T,
    tok_ref, cot_ref, win_ref, wout_ref,
    out_ref, gtok_ref, gin_ref, gout_ref,
    own, tc, win, wout, part, zsend, zrecv, hid, osend, orecv, gin, gout, ends,
    load_sem, gsend_sem, grecv_sem, zsend_sem, zrecv_sem, hsend_sem, hrecv_sem, osend_sem, orecv_sem, store_sem,
):
    row, z = lax.axis_index("row"), lax.axis_index("col")
    S = nz // 2
    J = S // 2

    def wrap(v):
        return jnp.where(v >= nz, v - nz, v)

    def plus(o):
        return wrap(row + o)

    def minus(o):
        return wrap(row - o + nz)

    def owner(p):
        if isinstance(p, int):
            k = S - p // 2 if p % 2 == 0 else nz + (p + 1) // 2 - S
            return wrap(z + k % nz)
        half = lax.div(p + 1, 2)
        return wrap(z + jnp.where(lax.rem(p, 2) == 0, S - half, wrap(half - S + nz)))

    def rows(p, n=1):
        return pl.ds(pl.multiple_of(p * T, T), n * T)

    side = (wrap(z + 1), wrap(z + nz - 1))
    far = (wrap(z + 2), wrap(z + nz - 2))
    ring = side + (far if nz > 4 else far[:1])

    for i, (src, dst) in enumerate(
        ((tok_ref, own.at[0]), (cot_ref, own.at[1]), (win_ref, win), (wout_ref, wout))
    ):
        pltpu.make_async_copy(src, dst, load_sem.at[i]).start()

    barrier = pltpu.get_barrier_semaphore()
    for peer in ring:
        pl.semaphore_signal(barrier, inc=1, device_id=(row, peer), device_id_type=MESH)

    @pl.loop(1, nz)
    def _(o):
        pl.semaphore_signal(barrier, inc=1, device_id=(plus(o), z), device_id_type=MESH)

    for i, (src, dst) in enumerate(((tok_ref, own.at[0]), (cot_ref, own.at[1]))):
        pltpu.make_async_copy(src, dst, load_sem.at[i]).wait()
    pl.semaphore_wait(barrier, nz - 1 + len(ring))

    def gather(p, peer):
        return pltpu.make_async_remote_copy(
            src_ref=own, dst_ref=tc.at[:, rows(p)],
            send_sem=gsend_sem.at[p], recv_sem=grecv_sem.at[p],
            device_id=(peer, z), device_id_type=MESH,
        )

    def gather_self(p):
        return pltpu.make_async_copy(own, tc.at[:, rows(p)], grecv_sem.at[p])

    def spread(lo, n):
        for k in range(n):
            p = lo + k
            o = owner(p)

            @pl.when(o != 0)
            def _():
                gather(p, minus(o)).start()

            @pl.when(o == 0)
            def _():
                gather_self(p).start()

    spread(0, min(8, nz))
    for i, (src, dst) in ((2, (win_ref, win)), (3, (wout_ref, wout))):
        pltpu.make_async_copy(src, dst, load_sem.at[i]).wait()

    def partials(j):
        for k in range(4):
            gather_self(4 * j + k).wait()
        r = rows(4 * j, 4)
        part[0, r, :] = mm(tc[0, r, :], win[...], NN)
        part[1, r, :] = mm(tc[1, r, :], wout[...], NT)

    def zcopy(d, i, slot, peer):
        return pltpu.make_async_remote_copy(
            src_ref=zsend.at[d, i, rows(slot)], dst_ref=zrecv.at[d, i, rows(slot)],
            send_sem=zsend_sem.at[d, i, slot], recv_sem=zrecv_sem.at[d, i, slot],
            device_id=(row, peer[d]), device_id_type=MESH,
        )

    def znext(d, j):
        return pltpu.make_async_remote_copy(
            src_ref=zsend.at[d, :, rows(J + j)], dst_ref=zrecv.at[d, :, rows(J + j)],
            send_sem=zsend_sem.at[d, 0, J + j], recv_sem=zrecv_sem.at[d, 0, J + j],
            device_id=(row, side[d]), device_id_type=MESH,
        )

    def beside(d, i, j):
        if i == 0:
            znext(d, j).wait_recv()
        return decode(zrecv[d, i, rows(J + j), :])

    def arrived(d, i, slot):
        zcopy(d, i, slot, side).wait_recv()
        return decode(zrecv[d, i, rows(slot), :])

    def zfar(j, first):
        for i in range(2):
            for d in range(2):
                if first == 0 and d == 1:
                    continue
                value = part[i, rows(4 * j - d), :]
                if first > 0:
                    value = value + beside(d, i, j - 1)
                if first > d:
                    value = value + arrived(d, i, j - 1)
                zsend[d, i, rows(j), :] = encode(value)
                zcopy(d, i, j, far).start()

    def znear(j):
        for d in range(2):
            for i in range(2):
                zsend[d, i, rows(J + j), :] = encode(part[i, rows(4 * j + 2 - d), :])
            znext(d, j).start()

    def zstep(j, first):
        partials(j)
        znear(j)
        zfar(j, first)

    partials(0)
    zfar(0, 0)
    znear(0)
    if J > 2:
        spread(8, 4)
    if J > 1:
        zstep(1, 1)
    if J > 2:
        if J > 3:
            spread(12, 4)

        @pl.loop(2, J)
        def _(j):
            @pl.when(j < J - 2)
            def _():
                spread(4 * j + 8, 4)

            zstep(j, 2)

    def hslot(d, k):
        return 2 * (S - k) - 1 + (d if k else 0)

    def hfar(d, i, j):
        return pltpu.make_async_remote_copy(
            src_ref=hid.at[i, rows(hslot(d, 2 * j))], dst_ref=hid.at[i, rows(hslot(d, 2 * j + 2))],
            send_sem=hsend_sem.at[d, i, j], recv_sem=hrecv_sem.at[d, i, j],
            device_id=(row, far[d]), device_id_type=MESH,
        )

    def hnear(d, j):
        return pltpu.make_async_remote_copy(
            src_ref=hid.at[:, rows(hslot(d, 2 * j))], dst_ref=hid.at[:, rows(hslot(d, 2 * j + 1))],
            send_sem=hsend_sem.at[d, 0, J + j], recv_sem=hrecv_sem.at[d, 0, J + j],
            device_id=(row, side[d]), device_id_type=MESH,
        )

    def last(d):
        return J - 1 + d

    def forward(i, j):
        for d in (1, 0):
            if j > 0 and j <= last(d):
                hfar(d, i, j - 1).wait_recv()
            if j < last(d):
                hfar(d, i, j).start()
            if j < J and i == 1:
                hnear(d, j).start()

    own_rows = rows(nz - 1)
    slope = None
    for i in range(2):
        value = part[i, own_rows, :]
        for d in range(2):
            value = value + beside(d, i, J - 1)
            if J - 1 >= d:
                value = value + arrived(d, i, J - 1)
        if i == 0:
            value, slope = gelu_both(value)
        else:
            value = value * slope
        hid[i, own_rows, :] = value.astype(BF)
        forward(i, 0)

    def ocopy(p, peer):
        return pltpu.make_async_remote_copy(
            src_ref=osend.at[:, rows(p)], dst_ref=orecv.at[:, rows(p)],
            send_sem=osend_sem.at[p], recv_sem=orecv_sem.at[p],
            device_id=(peer, z), device_id_type=MESH,
        )

    def ocopy_self(p):
        return pltpu.make_async_copy(osend.at[:, rows(p)], orecv.at[:, rows(p)], orecv_sem.at[p])

    def products(lo, hi):
        r = slice(lo * T, hi * T)
        osend[0, r, :] = mm(hid[0, r, :], wout[...], NN).astype(BF)
        osend[1, r, :] = mm(hid[1, r, :], win[...], NT).astype(BF)

        for p in reversed(range(lo, hi)):
            o = owner(p)

            @pl.when(o != 0)
            def _():
                ocopy(p, plus(o)).start()

            @pl.when(o == 0)
            def _():
                ocopy_self(p).start()

    W = 128
    pieces = [(0, k) for k in range(gout_ref.shape[0] // W)] + [(1, k) for k in range(gin_ref.shape[0] // W)]
    half = nz // 2 * T

    def grad_piece(piece, r, add):
        which, k = piece
        c = slice(k * W, (k + 1) * W)
        if which == 0:
            ref, value = gout, mm(hid[0, r, c], tc[1, r, :], TN)
        else:
            ref, value = gin, mm(tc[0, r, c], hid[1, r, :], TN)
        ref[c, :] = ref[c, :] + value if add else value

    top = nz
    waiting = list(pieces)
    near = 0

    def ready(n):
        nonlocal near
        for k in range(near, n):
            for d in range(2):
                hnear(d, k).wait_recv()
        near = n

    def multiply(low):
        nonlocal top
        if low < top:
            products(low, top)
            top = low

    def left(j):
        if j == 1:
            @pl.loop(0, nz)
            def _(p):
                @pl.when(owner(p) != 0)
                def _():
                    gather(p, row).wait_send()
        if 2 <= j <= 3 or J < 3 and j == J:
            for d in ((0, 1) if J < 3 else (j - 2,)):
                pl.loop(0, J)(lambda j: znext(d, j).wait_send())
                for i in range(2):
                    pl.loop(d, J)(lambda slot: zcopy(d, i, slot, far).wait_send())

    def passed(j):
        for i in range(2):
            for d in range(2):
                if j < J and i == 0:
                    hnear(d, j).wait_send()
                if j < last(d):
                    hfar(d, i, j).wait_send()

    for j in range(1, J + 1):
        for i in range(2):
            forward(i, j)
        if j > 1:
            ready(j - 1)
            multiply(nz - 1 - 4 * (j - 1))
        if top <= nz // 2 and j < J:
            for piece in waiting[:4]:
                grad_piece(piece, slice(half, 2 * half), False)
            waiting = waiting[4:]
        left(j)
        if j > 2:
            passed(j - 3)
    ready(J)
    multiply(0)
    for piece in waiting:
        grad_piece(piece, slice(half, 2 * half), False)

    stores = []

    def put(src, dst):
        stores.append(pltpu.make_async_copy(src, dst, store_sem.at[len(stores)]))
        stores[-1].start()

    for piece in pieces:
        grad_piece(piece, slice(0, half), True)
        c = slice(piece[1] * W, (piece[1] + 1) * W)
        if piece[0] == 0:
            put(gout.at[c], gout_ref.at[c])
        else:
            put(gin.at[c], gin_ref.at[c])

    for p in reversed(range(nz)):
        ocopy_self(p).wait()
    for i, ref in enumerate((out_ref, gtok_ref)):
        total = own[i].astype(F32)
        for p in range(nz):
            total = total + orecv[i, rows(p), :].astype(F32)
        ends[i] = total.astype(BF)
        put(ends.at[i], ref)

    for j in range(max(J - 2, 0), J):
        passed(j)

    @pl.loop(0, nz)
    def _(p):
        @pl.when(owner(p) != 0)
        def _():
            ocopy(p, row).wait_send()

    for copy in stores:
        copy.wait()


def store(*refs):
    sources, targets, held, sems = refs[:4], refs[4:8], refs[8:12], refs[12]
    moves = []
    for source, target, block in zip(sources, targets, held):
        height = min(128, source.shape[0])
        for top in range(0, source.shape[0], height):
            c, n = pl.ds(top, height), len(moves)
            moves.append(
                (
                    pltpu.make_async_copy(source.at[c], block.at[c], sems.at[0, n]),
                    pltpu.make_async_copy(block.at[c], target.at[c], sems.at[1, n]),
                )
            )
    for load, _ in moves:
        load.start()
    for load, save in moves:
        load.wait()
        save.start()
    for _, save in moves:
        save.wait()


def on_device(nz, tokens, w_in, w_out, cotangent):
    T, DL = tokens.shape
    HL = w_in.shape[1]
    S = nz // 2
    hbm = pl.BlockSpec(memory_space=pltpu.HBM)
    dma = pltpu.SemaphoreType.DMA
    flops = 2 * 6 * nz * T * DL * HL
    outs = (
        jax.ShapeDtypeStruct((T, DL), BF),
        jax.ShapeDtypeStruct((T, DL), BF),
        jax.ShapeDtypeStruct((DL, HL), F32),
        jax.ShapeDtypeStruct((HL, DL), F32),
    )
    results = pl.pallas_call(
        functools.partial(kernel, nz, T),
        out_shape=outs,
        in_specs=[hbm] * 4,
        out_specs=(hbm,) * 4,
        scratch_shapes=[
            pltpu.VMEM((2, T, DL), BF),
            pltpu.VMEM((2, nz * T, DL), BF),
            pltpu.VMEM((DL, HL), BF),
            pltpu.VMEM((HL, DL), BF),
            pltpu.VMEM((2, nz * T, HL), F32),
            pltpu.VMEM((2, 2, S * T, HL), BF),
            pltpu.VMEM((2, 2, S * T, HL), BF),
            pltpu.VMEM((2, nz * T, HL), BF),
            pltpu.VMEM((2, nz * T, DL), BF),
            pltpu.VMEM((2, nz * T, DL), BF),
            pltpu.VMEM((DL, HL), F32),
            pltpu.VMEM((HL, DL), F32),
            pltpu.VMEM((2, T, DL), BF),
            dma((4,)),
            dma((nz,)),
            dma((nz,)),
            dma((2, 2, S)),
            dma((2, 2, S)),
            dma((2, 2, S)),
            dma((2, 2, S)),
            dma((nz,)),
            dma((nz,)),
            dma((2 + (DL + HL) // 128,)),
        ],
        compiler_params=pltpu.CompilerParams(
            collective_id=0, has_side_effects=True, vmem_limit_bytes=58 * 2**20
        ),
        cost_estimate=pl.CostEstimate(flops=flops, bytes_accessed=4 * DL * HL * 3, transcendentals=0),
    )(tokens, cotangent, w_in, w_out)
    return pl.pallas_call(
        store,
        out_shape=outs,
        in_specs=[pl.BlockSpec(memory_space=pl.ANY)] * 4,
        out_specs=(hbm,) * 4,
        scratch_shapes=[pltpu.VMEM(out.shape, out.dtype) for out in outs] + [dma((2, 2 + (DL + HL) // 128))],
        compiler_params=pltpu.CompilerParams(vmem_limit_bytes=58 * 2**20),
    )(*results)


def solution(mesh):
    nz = mesh.shape["col"]
    return jax.shard_map(
        functools.partial(on_device, nz),
        mesh=mesh,
        in_specs=(P("row", "col"), P("col", "row"), P("row", "col"), P("row", "col")),
        out_specs=(P("row", "col"), P("row", "col"), P("col", "row"), P("row", "col")),
        check_vma=False,
    )
```
